32 devices in a mesh: pipe: 8 (over z, y), expert: 4 (over x, core).
Axes of the slice: x: 2, y: 2, z: 4, core: 2. Of those that a mesh axis runs over, the one named last changes fastest.
Arguments:
- up_in: bfloat16 [8, 256, 2560], P('pipe', 'expert'), may hold values from -6 to 6
- down_in: bfloat16 [8, 256, 2560], P('pipe', 'expert'), may hold values from -6 to 6
- up_ids: int32 [8, 256, 6], P('pipe', 'expert'), may hold values from 0 to 15, all different within a row; in each aligned block of 64 rows (0 to 63, 64 to 127, ..., all dimensions but the last counted through in order) at most 32 rows name the same one
- down_ids: int32 [8, 256, 6], P('pipe', 'expert'), may hold values from 0 to 15, all different within a row; in each aligned block of 64 rows (0 to 63, 64 to 127, ..., all dimensions but the last counted through in order) at most 32 rows name the same one
- norm_gain: float32 [8, 2560], P('pipe'), may hold values from 0.1 to 1.9
- router: bfloat16 [8, 2560, 16], P('pipe'), may hold values from -0.25 to 0.25
- w_up: bfloat16 [8, 16, 2560, 1152], P('pipe', 'expert'), may hold values from -0.125 to 0.125
- w_down: bfloat16 [8, 16, 1152, 2560], P('pipe', 'expert'), may hold values from -0.375 to 0.375
Outputs:
- up_out: bfloat16 [8, 256, 2560], P('pipe', 'expert')
- down_out: bfloat16 [8, 256, 2560], P('pipe', 'expert')
The draws below stay inside these ranges and needn't reach their ends.
Inputs may be any that keep to these rules, and one draw needn't show every extreme that they name: `up_ids`: each token names 6 different experts. Within the tokens of one device (aligned blocks of 64 tokens of one section) no expert is named more than 32 times, and in every draw some expert is named exactly 32 times in some block. `down_ids`: as for up_ids.
All inputs are finite; a program needn't handle non-finite values.
Results may differ from the reference program's by a relative error of at most 0.0061.
Values may be sent and summed in bfloat16 or wider, within the bound.
A program may use at most 128 MiB of HBM per device.

```python
import math
import jax
import jax.numpy as jnp
import numpy as np
from jax import lax

D = 2560
FFW = 1152
EXPERTS = 16
TOP = 6
TOK_DEV = 64
CAP = 32
SECTIONS = 8
TOKENS = 256
N_EXPERT = 4


def block_levels(key, extent, cuts, least, largest):
    level, own = 1.0, jax.random.fold_in(key, 6)
    for dim, blocks in cuts:
        draws = jnp.exp(jax.random.uniform(jax.random.fold_in(own, dim), (blocks,), jnp.float32, least / len(cuts), largest / len(cuts)))
        level = level * jnp.repeat(draws, extent[dim] // blocks).reshape([-1 if axis == dim else 1 for axis in range(len(extent))])
    return level


def assign_block(rng, own, number, rows, number_of, top, limit, lean):
    order = jax.random.permutation(rng, number_of)
    heavy_load, common = load_shares(number_of, rows * top, limit, lean, True), load_shares(number_of, rows * top, limit, lean, False)
    places = jnp.arange(number_of)

    def named(lengths, rotation):
        used = int((lengths > 0).sum())
        fixed = max(1, used // 4)
        shifted = fixed + (places - fixed + rotation * (used - fixed)) % max(1, number_of - fixed)
        return jnp.zeros((number_of,), jnp.int32).at[order[jnp.where(places < fixed, places, shifted)]].set(jnp.asarray(lengths, jnp.int32))

    lengths = jnp.where(number % 4 == 0, named(heavy_load, number // 4), named(common, number - number // 4 - 1))
    mixed = jax.random.permutation(jax.random.fold_in(own, 3), number_of)
    source_of, taker = mixed[0:number_of // 2 * 2:2], mixed[1:number_of // 2 * 2:2]
    slack = jnp.minimum(lengths[source_of] - 1, limit - lengths[taker]) // 2
    slack = jnp.where((source_of == order[0]) | (taker == order[0]) | (lengths[taker] == 0), 0, jnp.maximum(slack, 0))
    shifted = jax.random.randint(jax.random.fold_in(own, 4), (number_of // 2,), 0, 1 << 20) % (slack + 1)
    lengths = lengths.at[source_of].add(-shifted).at[taker].add(shifted)
    members = jnp.searchsorted(jnp.cumsum(lengths), jnp.arange(rows * top), side="right").astype(jnp.int32)
    listing = members.reshape(top, rows).T
    listing = listing[jax.random.permutation(jax.random.fold_in(own, 1), rows)]
    rotation = jax.random.randint(jax.random.fold_in(own, 2), (rows, 1), 0, top)
    return jnp.take_along_axis(listing, (jnp.arange(top)[None, :] + rotation) % top, axis=1)


def load_shares(count, total, limit, skew, full):
    weights = [(1 << 20) // math.isqrt(rank ** skew) + 1 for rank in range(1, count + 1)]
    largest = limit if full else min(limit, max(-(-total // count), total * weights[0] // sum(weights)))
    least = 1 if total - largest >= count - 1 else 0
    holding, rest = [largest] + [least] * (count - 1), total - largest - least * (count - 1)
    while rest > 0:
        candidates = [i for i in range(1, count) if holding[i] < largest] or [i for i in range(1, count) if holding[i] < limit]
        mass, budget = sum([weights[i] for i in candidates]), rest
        for i in candidates:
            addition = min(limit - holding[i], max(1, budget * weights[i] // mass), rest)
            holding[i] = holding[i] + addition
            rest = rest - addition
    return np.array(holding)


def gaussian(own_key, extent, scale, reach, shards=(), kind=jnp.bfloat16):
    loudness = block_levels(own_key, extent, shards, -0.22, 0.18) if shards else 1.0
    entries = jax.random.normal(own_key, extent, jnp.float32) * scale * loudness
    return jnp.minimum(jnp.maximum(entries, -reach), reach).astype(kind)


def setup_inputs(seed: int = 0) -> dict:
    key_of = jax.random.split(jax.random.key(seed), 9)
    up_in = gaussian(key_of[0], (SECTIONS, TOKENS, D), 1.0, 6.0, ((0, 8), (1, 4)))
    down_in = gaussian(key_of[1], (SECTIONS, TOKENS, D), 1.0, 6.0, ((0, 8), (1, 4)))
    up_ids_keys = jax.random.split(jax.random.fold_in(key_of[2], 1), SECTIONS * TOKENS // TOK_DEV)
    up_ids_turns = jax.random.permutation(jax.random.fold_in(key_of[2], 3), SECTIONS * TOKENS // TOK_DEV)
    up_ids = jax.vmap(lambda own, number: assign_block(jax.random.fold_in(key_of[2], 2), own, number, TOK_DEV, EXPERTS, TOP, CAP, 2))(up_ids_keys, up_ids_turns).reshape((SECTIONS, TOKENS, TOP))
    down_ids_keys = jax.random.split(jax.random.fold_in(key_of[3], 1), SECTIONS * TOKENS // TOK_DEV)
    down_ids_turns = jax.random.permutation(jax.random.fold_in(key_of[3], 3), SECTIONS * TOKENS // TOK_DEV)
    down_ids = jax.vmap(lambda own, number: assign_block(jax.random.fold_in(key_of[3], 2), own, number, TOK_DEV, EXPERTS, TOP, CAP, 2))(down_ids_keys, down_ids_turns).reshape((SECTIONS, TOKENS, TOP))
    norm_gain = jnp.clip(1.0 + 0.18 * jax.random.normal(key_of[4], (SECTIONS, D), jnp.float32), 0.1, 1.9)
    router = gaussian(key_of[5], (SECTIONS, D, EXPERTS), (D // 4) ** -0.5, 0.25, ((0, 8),))
    w_up = gaussian(key_of[6], (SECTIONS, EXPERTS, D, FFW), D ** -0.5, 0.125, ((0, 8), (1, 4)))
    w_down = gaussian(key_of[7], (SECTIONS, EXPERTS, FFW, D), (FFW // 4) ** -0.5, 0.375, ((0, 8), (1, 4)))
    return {"up_in": up_in, "down_in": down_in, "up_ids": up_ids, "down_ids": down_ids, "norm_gain": norm_gain, "router": router, "w_up": w_up, "w_down": w_down}


def norm_route(x, ids, gain, table):
    xf = x.astype(jnp.float32)
    normed = (xf * lax.rsqrt(lax.optimization_barrier(jnp.mean(xf * xf, axis=-1, keepdims=True)) + 1e-06) * gain).astype(jnp.bfloat16)
    logits = jnp.dot(normed, table, preferred_element_type=jnp.float32)
    chosen = jnp.take_along_axis(logits, ids, axis=1)
    score = jax.nn.sigmoid(chosen)
    gates = score / lax.optimization_barrier(jnp.sum(score, axis=-1, keepdims=True))
    return (normed, gates)

def one_expert(packed):
    rows, up_w, down_w = packed
    up_h = jnp.dot(rows, up_w, preferred_element_type=jnp.float32)
    hidden = jax.nn.silu(up_h).astype(jnp.bfloat16)
    return jnp.dot(hidden, down_w, preferred_element_type=jnp.float32).astype(jnp.bfloat16)

def moe_layer(x, ids, gain, table, up_w, down_w):
    normed, gates = norm_route(x, ids, gain, table)
    blocks = N_EXPERT
    per_block = ids.reshape(blocks, TOK_DEV * TOP)
    onehot = (per_block[:, :, None] == jnp.arange(EXPERTS, dtype=jnp.int32)[None, None, :]).astype(jnp.int32)
    before = jnp.cumsum(onehot, axis=1) - onehot
    slot = lax.optimization_barrier(jnp.sum(before * onehot, axis=-1))
    source = jnp.arange(blocks, dtype=jnp.int32)[:, None]
    target = (per_block * (blocks * CAP) + source * CAP + slot).reshape(-1).astype(jnp.int32)
    repeated = jnp.repeat(normed, TOP, axis=0)
    buffer = jnp.zeros((EXPERTS * blocks * CAP, D), jnp.bfloat16).at[target].set(repeated)
    outputs = lax.map(one_expert, (buffer.reshape(EXPERTS, blocks * CAP, D), up_w, down_w))
    picked = jnp.take(outputs.reshape(EXPERTS * blocks * CAP, D), target, axis=0)
    picked = picked.reshape(TOKENS, TOP, D).astype(jnp.float32)
    combined = lax.optimization_barrier(jnp.sum(gates[:, :, None] * picked, axis=1))
    return (x.astype(jnp.float32) + 2.5 * combined).astype(jnp.bfloat16)

def one_section(packed):
    x_up, ids_up, x_down, ids_down, gain, table, up_w, down_w = packed
    out_up = moe_layer(x_up, ids_up, gain, table, up_w, down_w)
    out_down = moe_layer(x_down, ids_down, gain, table, up_w, down_w)
    return (out_up, out_down)

def reference(up_in, down_in, up_ids, down_ids, norm_gain, router, w_up, w_down):
    layer_up, layer_down = lax.map(one_section, (up_in, up_ids, down_in, down_ids, norm_gain, router, w_up, w_down))
    return (jnp.roll(layer_up, 1, axis=0), jnp.roll(layer_down, -1, axis=0))
```

```python
import jax
import jax.numpy as jnp
from jax import lax
from jax.sharding import PartitionSpec as P

CAP = 32


def shifted(block, axis, distance):
    devices = range(lax.axis_size(axis))
    route = [((i - distance) % len(devices), i) for i in devices]
    return lax.ppermute(block, axis, route)


def layer(x, ids, gain, table, up_w, down_w):
    here, width = x.shape
    experts = table.shape[1]
    local = up_w.shape[0]
    owners = experts // local
    xf = x.astype(jnp.float32)
    normed = (xf * lax.rsqrt(jnp.mean(xf * xf, axis=-1, keepdims=True) + 1e-06) * gain).astype(
        jnp.bfloat16
    )
    logits = jnp.dot(normed, table, preferred_element_type=jnp.float32)
    onehot = ids[:, :, None] == jnp.arange(experts, dtype=jnp.int32)[None, None, :]
    chosen = jnp.any(onehot, axis=1)
    score = jnp.where(chosen, jax.nn.sigmoid(logits), 0.0)
    gates = score / jnp.sum(score, axis=-1, keepdims=True)
    everyone = lax.all_gather(normed, "expert", axis=0, tiled=True)
    weights = lax.all_to_all(
        gates.reshape(here, owners, local).transpose(1, 0, 2), "expert", 0, 0, tiled=False
    ).reshape(owners, here, local)
    taken = (weights > 0).astype(jnp.float32)
    lower = (jnp.arange(here)[:, None] > jnp.arange(here)[None, :]).astype(jnp.float32)
    slot = jnp.einsum("tu,oul->otl", lower, taken)
    place = (
        (slot[:, :, :, None] == jnp.arange(CAP, dtype=jnp.float32)) & (weights > 0)[..., None]
    )
    hot = place.astype(jnp.bfloat16)
    rows = jnp.einsum(
        "otlc,otd->locd",
        hot,
        everyone.reshape(owners, here, width),
        preferred_element_type=jnp.float32,
    ).astype(jnp.bfloat16)
    rows = rows.reshape(local, owners * CAP, width)
    up_h = jnp.einsum("lcd,ldf->lcf", rows, up_w, preferred_element_type=jnp.float32)
    hidden = jax.nn.silu(up_h).astype(jnp.bfloat16)
    out = jnp.einsum("lcf,lfd->lcd", hidden, down_w, preferred_element_type=jnp.float32)
    row_gate = jnp.einsum("otlc,otl->loc", place.astype(jnp.float32), weights)
    scaled = (out * (2.5 * row_gate).reshape(local, owners * CAP, 1)).astype(jnp.bfloat16)
    part = jnp.einsum(
        "otlc,locd->otd",
        hot,
        scaled.reshape(local, owners, CAP, width),
        preferred_element_type=jnp.float32,
    ).astype(jnp.bfloat16)
    mine = lax.psum_scatter(part, "expert", scatter_dimension=0, tiled=True)[0]
    return (xf + mine.astype(jnp.float32)).astype(jnp.bfloat16)


def per_device(up_in, down_in, up_ids, down_ids, norm_gain, router, w_up, w_down):
    args = (norm_gain[0], router[0], w_up[0], w_down[0])
    up = layer(up_in[0], up_ids[0], *args)
    down = layer(down_in[0], down_ids[0], *args)
    return (shifted(up[None], "pipe", 1), shifted(down[None], "pipe", -1))


def solution(mesh):
    token = P("pipe", "expert", None)
    placed = (
        token,
        token,
        token,
        token,
        P("pipe", None),
        P("pipe", None, None),
        P("pipe", "expert", None, None),
        P("pipe", "expert", None, None),
    )
    return jax.shard_map(
        per_device, mesh=mesh, in_specs=placed, out_specs=(token, token), check_vma=False
    )
```

```python
import functools

import jax
import jax.numpy as jnp
from jax import lax
from jax.experimental import pallas as pl
from jax.experimental.pallas import tpu as pltpu
from jax.sharding import PartitionSpec as P

CAP = 32
EXTRA = 128
MESH = pl.DeviceIdType.MESH
BF16, F32 = jnp.bfloat16, jnp.float32


def kernel(
    owners,
    pipes,
    columns,
    up_ref,
    down_ref,
    up_ids,
    down_ids,
    gain_ref,
    router_ref,
    w_up,
    w_down,
    up_out,
    down_out,
    tokens,
    rows,
    hidden,
    spread,
    scaled,
    part,
    paired,
    crossed,
    final,
    wu,
    wd,
    wu_sem,
    wd_sem,
    own_send,
    own_recv,
    far_send,
    far_recv,
    fwd_send,
    fwd_recv,
    pair_send,
    pair_recv,
    cross_send,
    cross_recv,
    out_send,
    out_recv,
):
    chips = owners // 2
    here, width = up_ref.shape[1:]
    experts = router_ref.shape[2]
    local = w_up.shape[1]
    slots = owners * CAP
    everyone = owners * here
    chunks = width // columns
    pipe, me = lax.axis_index("pipe"), lax.axis_index("expert")
    chip, core = me // 2, lax.rem(me, 2)
    other = 1 - core
    sibling = {"expert": chip * 2 + other}
    above = {"pipe": lax.rem(pipe + 1, pipes)}
    below = {"pipe": lax.rem(pipe + pipes - 1, pipes)}

    def across(k):
        return lax.rem(chip + k, chips)

    def facing(k):
        return {"expert": across(k) * 2 + core}

    def cols(c):
        return pl.ds(pl.multiple_of(c * columns, columns), columns)

    def load_up(l):
        return pltpu.make_async_copy(w_up.at[0, l], wu.at[l], wu_sem.at[l])

    def load_down(c):
        return pltpu.make_async_copy(
            w_down.at[0, :, :, cols(c)], wd.at[:, :, cols(c)], wd_sem.at[c]
        )

    def remote(src, dst, send, recv, to):
        return pltpu.make_async_remote_copy(
            src_ref=src,
            dst_ref=dst,
            send_sem=send,
            recv_sem=recv,
            device_id=to,
            device_id_type=MESH,
        )

    def own_copy(d):
        block = tokens.at[d, core, chip]
        return remote(block, block, own_send.at[d], own_recv.at[d], sibling)

    def far_copy(d, k):
        block = tokens.at[d, core, chip]
        return remote(block, block, far_send.at[d, k - 1], far_recv.at[d, k - 1], facing(k))

    def fwd_copy(d, k):
        block = tokens.at[d, core, across(chips - k)]
        return remote(block, block, fwd_send.at[d, k - 1], fwd_recv.at[d, k - 1], sibling)

    def pair_copy(d, c):
        return remote(
            part.at[d, other, :, :, cols(c)],
            paired.at[d, :, :, cols(c)],
            pair_send.at[d, c],
            pair_recv.at[d, c],
            sibling,
        )

    def cross_copy(d, c, k):
        return remote(
            part.at[d, core, across(k), :, cols(c)],
            crossed.at[d, k - 1, :, cols(c)],
            cross_send.at[d, c, k - 1],
            cross_recv.at[d, c, k - 1],
            facing(k),
        )

    def out_copy(d, c):
        target, to = ((up_out, above), (down_out, below))[d]
        return remote(
            final.at[d, :, cols(c)],
            target.at[0, :, cols(c)],
            out_send.at[d, c],
            out_recv.at[d, c],
            to,
        )

    for l in range(local):
        load_up(l).start()

    barrier = pltpu.get_barrier_semaphore()
    partners = [sibling, above, below] + [facing(k) for k in range(1, chips)]
    for partner in partners:
        pl.semaphore_signal(barrier, inc=1, device_id=partner, device_id_type=MESH)

    def route(d):
        x_ref, ids_ref = ((up_ref, up_ids), (down_ref, down_ids))[d]
        xf = x_ref[0].astype(F32)
        mean = jnp.mean(xf * xf, axis=-1, keepdims=True)
        normed = (xf * lax.rsqrt(mean + 1e-06) * gain_ref[...]).astype(BF16)
        logits = jnp.dot(normed, router_ref[0], preferred_element_type=F32)
        ids = ids_ref[0]
        lane = lax.broadcasted_iota(jnp.int32, (here, experts), 1)
        taken = jnp.zeros((here, experts), F32)
        for k in range(ids.shape[1]):
            taken = taken + jnp.where(ids[:, k : k + 1] == lane, 1.0, 0.0)
        score = taken / (1.0 + jnp.exp(-logits))
        gates = 2.5 * (score / jnp.sum(score, axis=-1, keepdims=True))
        high = gates.astype(BF16)
        low = (gates - high.astype(F32)).astype(BF16)
        earlier = lax.broadcasted_iota(jnp.int32, (here, here), 0) > lax.broadcasted_iota(
            jnp.int32, (here, here), 1
        )
        slot = jnp.dot(
            jnp.where(earlier, 1.0, 0.0).astype(BF16),
            taken.astype(BF16),
            preferred_element_type=F32,
        )
        slot = jnp.where(taken > 0.0, slot, -1024.0).astype(BF16)
        from_lane = lax.broadcasted_iota(jnp.int32, (experts, EXTRA), 0)
        to_lane = lax.broadcasted_iota(jnp.int32, (experts, EXTRA), 1)
        extra = jnp.zeros((here, EXTRA), F32)
        for place, value in enumerate((high, low, slot)):
            move = jnp.where(from_lane + place * experts == to_lane, 1.0, 0.0).astype(BF16)
            extra = extra + jnp.dot(value, move, preferred_element_type=F32)
        tokens[d, core, chip, :, :width] = normed
        tokens[d, core, chip, :, width:] = extra.astype(BF16)

    def find_rows(d):
        everything = tokens[d].reshape(everyone, width + EXTRA)
        extra = tokens[d, :, :, :, width:].reshape(everyone, EXTRA).astype(F32)
        lane = lax.broadcasted_iota(jnp.int32, (everyone, EXTRA), 1)
        block = lax.broadcasted_iota(jnp.int32, (everyone, slots), 0) // here
        place = lax.broadcasted_iota(jnp.int32, (everyone, slots), 1) - block * CAP

        @pl.loop(0, local)
        def _(l):
            column = 2 * experts + me * local + l
            slot = jnp.sum(jnp.where(lane == column, extra, 0.0), axis=1, keepdims=True)
            hot = jnp.where(place.astype(F32) == slot, 1.0, 0.0)
            spread[:, pl.ds(pl.multiple_of(l * slots, slots), slots)] = hot.astype(BF16)
            rows[l] = jnp.dot(
                hot.T.astype(BF16), everything, preferred_element_type=F32
            ).astype(BF16)

    def find_hidden(d):
        @pl.loop(0, local)
        def _(l):
            if d == 0:
                load_up(l).wait()
            up_h = jnp.dot(rows[l, :, :width], wu[l], preferred_element_type=F32)
            hidden[l] = (up_h / (1.0 + jnp.exp(-up_h))).astype(BF16)

    def find_part(d, c):
        if d == 0:
            load_down(c).wait()
        lane = lax.broadcasted_iota(jnp.int32, (slots, EXTRA), 1)
        for l in range(local):
            expert = me * local + l
            gate = jnp.sum(
                jnp.where(
                    (lane == expert) | (lane == expert + experts),
                    rows[l, :, width:].astype(F32),
                    0.0,
                ),
                axis=1,
                keepdims=True,
            )
            value = jnp.dot(hidden[l], wd[l, :, cols(c)], preferred_element_type=F32)
            scaled[l * slots : (l + 1) * slots, :] = (value * gate).astype(BF16)
        total = jnp.dot(spread[...], scaled[...], preferred_element_type=F32).astype(BF16)
        part[d, :, :, :, cols(c)] = total.reshape(2, chips, here, columns)
        pair_copy(d, c).start()

    def cross(d, c):
        pair_copy(d, c).wait_recv()
        for k in range(1, chips):
            q = across(k)
            both = part[d, core, q, :, cols(c)].astype(F32) + paired[d, q, :, cols(c)].astype(F32)
            part[d, core, q, :, cols(c)] = both.astype(BF16)
            cross_copy(d, c, k).start()

    def finish(d, c):
        x_ref = (up_ref, down_ref)[d]
        total = x_ref[0, :, cols(c)].astype(F32)
        total = total + part[d, core, chip, :, cols(c)].astype(F32)
        total = total + paired[d, chip, :, cols(c)].astype(F32)
        for k in range(1, chips):
            cross_copy(d, c, k).wait_recv()
            total = total + crossed[d, k - 1, :, cols(c)].astype(F32)
        final[d, :, cols(c)] = total.astype(BF16)
        out_copy(d, c).start()

    def forward(d):
        for k in range(1, chips):
            far_copy(d, k).wait_recv()
            fwd_copy(d, k).start()

    route(0)
    pl.semaphore_wait(barrier, len(partners))
    for k in range(1, chips):
        far_copy(0, k).start()
    own_copy(0).start()
    for c in range(chunks):
        load_down(c).start()
    route(1)
    own_copy(1).start()
    forward(0)
    for k in range(1, chips):
        far_copy(1, k).start()

    own_copy(0).wait_recv()
    for k in range(1, chips):
        fwd_copy(0, k).wait_recv()
    find_rows(0)
    find_hidden(0)

    @pl.loop(0, chunks)
    def _(c):
        find_part(0, c)

        @pl.when(c >= 1)
        def _():
            cross(0, c - 1)

        @pl.when(c == chunks - 2)
        def _():
            forward(1)

    cross(0, chunks - 1)
    own_copy(1).wait_recv()
    for k in range(1, chips):
        fwd_copy(1, k).wait_recv()
    find_rows(1)
    find_hidden(1)

    @pl.loop(0, chunks)
    def _(c):
        find_part(1, c)

        @pl.when(c >= 1)
        def _():
            cross(1, c - 1)

        finish(0, c)

    cross(1, chunks - 1)

    @pl.loop(0, chunks)
    def _(c):
        finish(1, c)

    for d in range(2):
        own_copy(d).wait_send()
        for k in range(1, chips):
            far_copy(d, k).wait_send()
            fwd_copy(d, k).wait_send()

        @pl.loop(0, chunks)
        def _(c):
            pair_copy(d, c).wait_send()
            for k in range(1, chips):
                cross_copy(d, c, k).wait_send()
            out_copy(d, c).wait_send()
            out_copy(d, c).wait_recv()


def solution(mesh):
    owners, pipes = mesh.shape["expert"], mesh.shape["pipe"]
    chips = owners // 2
    token = P("pipe", "expert", None)

    def per_device(up_in, down_in, up_ids, down_ids, norm_gain, router, w_up, w_down):
        here, width = up_in.shape[1:]
        local, _, inner = w_up.shape[1:]
        slots = owners * CAP
        columns = 512
        chunks = width // columns
        dma = pltpu.SemaphoreType.DMA
        shape = jax.ShapeDtypeStruct(up_in.shape, BF16)
        vmem = pl.BlockSpec(memory_space=pltpu.VMEM)
        hbm = pl.BlockSpec(memory_space=pl.ANY)
        return pl.pallas_call(
            functools.partial(kernel, owners, pipes, columns),
            out_shape=(shape, shape),
            in_specs=[vmem] * 6 + [hbm] * 2,
            out_specs=(hbm, hbm),
            scratch_shapes=[
                pltpu.VMEM((2, 2, chips, here, width + EXTRA), BF16),
                pltpu.VMEM((local, slots, width + EXTRA), BF16),
                pltpu.VMEM((local, slots, inner), BF16),
                pltpu.VMEM((owners * here, local * slots), BF16),
                pltpu.VMEM((local * slots, columns), BF16),
                pltpu.VMEM((2, 2, chips, here, width), BF16),
                pltpu.VMEM((2, chips, here, width), BF16),
                pltpu.VMEM((2, chips - 1, here, width), BF16),
                pltpu.VMEM((2, here, width), BF16),
                pltpu.VMEM((local, width, inner), BF16),
                pltpu.VMEM((local, inner, width), BF16),
                dma((local,)),
                dma((chunks,)),
                dma((2,)),
                dma((2,)),
                dma((2, chips - 1)),
                dma((2, chips - 1)),
                dma((2, chips - 1)),
                dma((2, chips - 1)),
                dma((2, chunks)),
                dma((2, chunks)),
                dma((2, chunks, chips - 1)),
                dma((2, chunks, chips - 1)),
                dma((2, chunks)),
                dma((2, chunks)),
            ],
            compiler_params=pltpu.CompilerParams(
                collective_id=0, has_side_effects=True, vmem_limit_bytes=63 * 1024 * 1024
            ),
        )(up_in, down_in, up_ids, down_ids, norm_gain, router, w_up, w_down)

    return jax.shard_map(
        per_device,
        mesh=mesh,
        in_specs=(
            token,
            token,
            token,
            token,
            P("pipe", None),
            P("pipe", None, None),
            P("pipe", "expert", None, None),
            P("pipe", "expert", None, None),
        ),
        out_specs=(token, token),
        check_vma=False,
    )
```
